32 devices in a mesh: dp: 16 (over z, y, x), tensor: 2 (over core).
Axes of the slice: x: 2, y: 2, z: 4, core: 2. Of those that a mesh axis runs over, the one named last changes fastest.
Arguments:
- latents: bfloat16 [16, 1184, 1536], P('dp', 'tensor'), may hold values from -6 to 6
- conditioning: bfloat16 [16, 1536], P('dp'), may hold values from -6 to 6
- valid_length: int32 [16], P('dp'), may hold values from 1025 to 1178, as said below
- cotangent: bfloat16 [16, 1184, 1536], P('dp', 'tensor'), may hold values from -6 to 6
- modulation: float32 [2, 1536, 9216], P(None, 'dp', 'tensor'), may hold values from -0.15625 to 0.15625
- attention: float32 [2, 1536, 3, 1536], P(None, 'dp', None, 'tensor'), may hold values from -0.15625 to 0.15625
- outward: float32 [2, 1536, 1536], P(None, 'tensor', 'dp'), may hold values from -1.25 to 1.25
- expand: float32 [2, 1536, 6144], P(None, 'dp', 'tensor'), may hold values from -0.15625 to 0.15625
- shrink: float32 [2, 6144, 1536], P(None, 'tensor', 'dp'), may hold values from -0.078125 to 0.078125
- modulation_moment: float32 [2, 1536, 9216], P(None, 'dp', 'tensor'), may hold values from -7104 to 7104
- attention_moment: float32 [2, 1536, 3, 1536], P(None, 'dp', None, 'tensor'), may hold values from -7104 to 7104
- outward_moment: float32 [2, 1536, 1536], P(None, 'tensor', 'dp'), may hold values from -6 to 6
- expand_moment: float32 [2, 1536, 6144], P(None, 'dp', 'tensor'), may hold values from -6 to 6
- shrink_moment: float32 [2, 6144, 1536], P(None, 'tensor', 'dp'), may hold values from -6 to 6
- modulation_average: float32 [2, 1536, 9216], P(None, 'dp', 'tensor'), may hold values from -0.15625 to 0.15625
- attention_average: float32 [2, 1536, 3, 1536], P(None, 'dp', None, 'tensor'), may hold values from -0.15625 to 0.15625
- outward_average: float32 [2, 1536, 1536], P(None, 'tensor', 'dp'), may hold values from -1.25 to 1.25
- expand_average: float32 [2, 1536, 6144], P(None, 'dp', 'tensor'), may hold values from -0.15625 to 0.15625
- shrink_average: float32 [2, 6144, 1536], P(None, 'tensor', 'dp'), may hold values from -0.078125 to 0.078125
Outputs:
- block_output: bfloat16 [16, 1184, 1536], P('dp', 'tensor')
- input_gradient: float32 [16, 1184, 1536], P('dp', 'tensor')
- conditioning_gradient: float32 [16, 1536], P('dp', 'tensor')
- modulation_updated: float32 [2, 1536, 9216], P(None, 'dp', 'tensor')
- modulation_momentum: float32 [2, 1536, 9216], P(None, 'dp', 'tensor')
- modulation_smoothed: float32 [2, 1536, 9216], P(None, 'dp', 'tensor')
- attention_updated: float32 [2, 1536, 3, 1536], P(None, 'dp', None, 'tensor')
- attention_momentum: float32 [2, 1536, 3, 1536], P(None, 'dp', None, 'tensor')
- attention_smoothed: float32 [2, 1536, 3, 1536], P(None, 'dp', None, 'tensor')
- outward_updated: float32 [2, 1536, 1536], P(None, 'tensor', 'dp')
- outward_momentum: float32 [2, 1536, 1536], P(None, 'tensor', 'dp')
- outward_smoothed: float32 [2, 1536, 1536], P(None, 'tensor', 'dp')
- expand_updated: float32 [2, 1536, 6144], P(None, 'dp', 'tensor')
- expand_momentum: float32 [2, 1536, 6144], P(None, 'dp', 'tensor')
- expand_smoothed: float32 [2, 1536, 6144], P(None, 'dp', 'tensor')
- shrink_updated: float32 [2, 6144, 1536], P(None, 'tensor', 'dp')
- shrink_momentum: float32 [2, 6144, 1536], P(None, 'tensor', 'dp')
- shrink_smoothed: float32 [2, 6144, 1536], P(None, 'tensor', 'dp')
The draws below stay inside these ranges and needn't reach their ends.
Inputs may be any that keep to these rules, and one draw needn't show every extreme that they name: `valid_length`: 1024 image tokens plus a count of valid text tokens; among the one consecutive sequence one has all 154 text tokens valid.
All inputs are finite; a program needn't handle non-finite values.
Results may differ from the reference program's by a relative error of at most 0.018.
The reference program's roundings to bfloat16 on the way count: a program that leaves them out, or rounds other values in their place, can miss the bound.
Values may be sent and summed in bfloat16 or wider, within the bound.
No kernel may reach another device: no remote copies, remote signals or barrier semaphores. Data moves between devices by JAX's collectives and lax.ppermute only.
A program may use at most 512 MiB of HBM per device.

```python
import math
import jax
import jax.numpy as jnp
from jax import lax

D = 1536
HEADS = 24
HEAD = 64
FF = 6144
IMG = 1024
TXT = 154
LEN = 1184
SEQ_DEV = 1
SEQS = 16


def draw_valid_length(key, part):
    key = jax.random.fold_in(key, 11)
    first, second = jax.random.split(key)
    text = jax.random.randint(first, (SEQS,), 1, TXT + 1)
    chosen = jax.random.randint(second, (SEQS // SEQ_DEV, 1), 0, SEQ_DEV)
    complete = (jnp.arange(SEQ_DEV)[None, :] == chosen).reshape(SEQS)
    return (jnp.where(complete, TXT, text) + IMG).astype(jnp.int32)


def moment_values(key, shape, spread):
    return spread * jax.random.truncated_normal(key, -6.0, 6.0, shape, jnp.float32)


def draw_modulation_moment(key, part):
    key = jax.random.fold_in(key, 23)
    spread = 1.5 * math.sqrt(SEQS * LEN)
    return moment_values(key, (2, D, 6 * D), spread)


def draw_attention_moment(key, part):
    key = jax.random.fold_in(key, 29)
    spread = 1.5 * math.sqrt(SEQS * LEN)
    return moment_values(key, (2, D, 3, D), spread)


def block_levels(stream_key, extent, cuts, low, largest):
    factor_of = 1.0
    for position, blocks in cuts:
        heights = jax.random.uniform(jax.random.fold_in(jax.random.fold_in(stream_key, 6), position), (blocks,), jnp.float32, low / len(cuts), largest / len(cuts))
        factor_of = factor_of * jnp.repeat(jnp.exp(heights), extent[position] // blocks).reshape((-1,) + (1,) * (len(extent) - 1 - position))
    return factor_of


def normal_values(stream_key, shape, width, reach, shards=(), held_as=jnp.bfloat16):
    values = jax.random.normal(stream_key, shape, jnp.float32) * width
    if len(shards) > 0:
        values = block_levels(stream_key, shape, shards, -0.22, 0.18) * values
    return jnp.clip(values, min=-reach, max=reach).astype(held_as)


def setup_inputs(seed: int = 0) -> dict:
    key_of = jax.random.split(jax.random.key(seed), 20)
    return {
        "latents": normal_values(key_of[0], (SEQS, LEN, D), 1.0, 6.0, ((0, 16), (1, 2))),
        "conditioning": normal_values(key_of[1], (SEQS, D), 1.0, 6.0, ((0, 16),)),
        "valid_length": draw_valid_length(jax.random.fold_in(key_of[19], 71), 0),
        "cotangent": normal_values(key_of[3], (SEQS, LEN, D), 1.0, 6.0, ((0, 16), (1, 2))),
        "modulation": normal_values(key_of[4], (2, D, 6 * D), D ** -0.5, 0.15625, ((1, 16), (2, 2)), jnp.float32),
        "attention": normal_values(key_of[5], (2, D, 3, D), D ** -0.5, 0.15625, ((1, 16), (3, 2)), jnp.float32),
        "outward": normal_values(key_of[6], (2, D, D), (D * 16 // LEN) ** -0.5, 1.25, ((1, 2), (2, 16)), jnp.float32),
        "expand": normal_values(key_of[7], (2, D, FF), D ** -0.5, 0.15625, ((1, 16), (2, 2)), jnp.float32),
        "shrink": normal_values(key_of[8], (2, FF, D), FF ** -0.5, 0.078125, ((1, 2), (2, 16)), jnp.float32),
        "modulation_moment": draw_modulation_moment(jax.random.fold_in(key_of[19], 71), 0),
        "attention_moment": draw_attention_moment(jax.random.fold_in(key_of[19], 71), 0),
        "outward_moment": normal_values(key_of[11], (2, D, D), (max(1, SEQS * LEN // 8000)), 6.0, ((1, 2), (2, 16)), jnp.float32),
        "expand_moment": normal_values(key_of[12], (2, D, FF), (max(1, SEQS * LEN // 8000)), 6.0, ((1, 16), (2, 2)), jnp.float32),
        "shrink_moment": normal_values(key_of[13], (2, FF, D), (max(1, SEQS * LEN // 8000)), 6.0, ((1, 2), (2, 16)), jnp.float32),
        "modulation_average": normal_values(key_of[14], (2, D, 6 * D), D ** -0.5, 0.15625, ((1, 16), (2, 2)), jnp.float32),
        "attention_average": normal_values(key_of[15], (2, D, 3, D), D ** -0.5, 0.15625, ((1, 16), (3, 2)), jnp.float32),
        "outward_average": normal_values(key_of[16], (2, D, D), (D * 16 // LEN) ** -0.5, 1.25, ((1, 2), (2, 16)), jnp.float32),
        "expand_average": normal_values(key_of[17], (2, D, FF), D ** -0.5, 0.15625, ((1, 16), (2, 2)), jnp.float32),
        "shrink_average": normal_values(key_of[18], (2, FF, D), FF ** -0.5, 0.078125, ((1, 2), (2, 16)), jnp.float32),
    }


EPSILON = 1e-06
RATE = 0.0005
MOMENTUM = 0.9
AVERAGING = 0.8
MASKED = -1000000000.0

@jax.custom_vjp
def low(v):
    return lax.optimization_barrier(v.astype(jnp.bfloat16)).astype(jnp.float32)

@jax.custom_vjp
def low_back(v):
    return v

def low_keep(v):
    return (low(v), None)

def low_pass(kept, grad):
    return (grad,)

def back_keep(v):
    return (v, None)

def back_low(kept, grad):
    return (low(grad),)
low.defvjp(low_keep, low_pass)
low_back.defvjp(back_keep, back_low)

def precise_dot(left, right):
    return jnp.dot(left, right, precision=lax.Precision.HIGHEST, preferred_element_type=jnp.float32)

def layer_norm(values):
    center = values - lax.optimization_barrier(jnp.mean(values, axis=-1, keepdims=True))
    spread = lax.optimization_barrier(jnp.mean(center * center, axis=-1, keepdims=True))
    return center * lax.rsqrt(spread + EPSILON)

def streams(rows, weight):
    return jnp.concatenate([precise_dot(rows[:IMG], weight[0]), precise_dot(rows[IMG:], weight[1])], axis=0)

def forward_one(latent, condition, length, modulation, attention, outward, expand, shrink):
    modulation = low(modulation)
    attention = low(attention)
    outward = low(outward)
    expand = low(expand)
    shrink = low(shrink)
    silu_low = low(jax.nn.silu(condition))
    mods = jnp.stack([precise_dot(silu_low, modulation[0]), precise_dot(silu_low, modulation[1])])
    is_image = (jnp.arange(LEN) < IMG)[:, None]

    def component(index):
        return jnp.where(is_image, mods[0, index * D:(index + 1) * D], mods[1, index * D:(index + 1) * D])
    shift_one, scale_one, gate_one, shift_two, scale_two, gate_two = [component(index) for index in range(6)]
    shaped_one = low(layer_norm(latent) * (1.0 + scale_one) + shift_one)
    packed = low(low_back(streams(shaped_one, attention.reshape(2, D, 3 * D))))
    split = packed.reshape(LEN, 3, HEADS, HEAD)
    queries, keys, values = (split[:, 0], split[:, 1], split[:, 2])
    scale = 1.0 / math.sqrt(HEAD)
    raw = low_back(jnp.einsum('qhe,khe->hqk', queries, keys, precision=lax.Precision.HIGHEST) * scale)
    allowed = jnp.arange(LEN) < length
    scores = jnp.where(allowed[None, None, :], raw, MASKED)
    peak = lax.optimization_barrier(jnp.max(scores, axis=-1, keepdims=True))
    expo = jnp.exp(scores - peak)
    probs = low(expo / lax.optimization_barrier(jnp.sum(expo, axis=-1, keepdims=True)))
    attended = jnp.einsum('hqk,khe->qhe', probs, values, precision=lax.Precision.HIGHEST)
    mixed = low(low_back(attended.reshape(LEN, D)))
    branch_one = low_back(streams(mixed, outward))
    middle = latent + gate_one * branch_one
    shaped_two = low(layer_norm(middle) * (1.0 + scale_two) + shift_two)
    hidden_pre = low_back(streams(shaped_two, expand))
    hidden = low(jax.nn.gelu(hidden_pre, approximate=True))
    branch_two = low_back(streams(hidden, shrink))
    return middle + gate_two * branch_two

def update_one(master, moment, average, summed):
    velocity = MOMENTUM * moment + summed
    updated = master - RATE * (summed + MOMENTUM * velocity)
    smoothed = AVERAGING * average + (1.0 - AVERAGING) * updated
    return (updated, velocity, smoothed)

def reference(latents, conditioning, valid_length, cotangent, modulation, attention, outward, expand, shrink, modulation_moment, attention_moment, outward_moment, expand_moment, shrink_moment, modulation_average, attention_average, outward_average, expand_average, shrink_average):
    masters = (modulation, attention, outward, expand, shrink)

    def one_sequence(carry, item):
        latent, condition, length, upstream = item

        def forward(latent_value, condition_value, *weights):
            return forward_one(latent_value, condition_value, length, *weights)
        result, pull = jax.vjp(forward, latent.astype(jnp.float32), condition.astype(jnp.float32), *masters)
        pulled = pull(upstream.astype(jnp.float32))
        totals = tuple((total + piece for total, piece in zip(carry, pulled[2:])))
        return (totals, (result.astype(jnp.bfloat16), pulled[0], pulled[1]))
    zeros = tuple((jnp.zeros_like(weight) for weight in masters))
    sums, (block_output, input_gradient, conditioning_gradient) = lax.scan(one_sequence, zeros, (latents, conditioning, valid_length, cotangent))
    modulation_updated, modulation_momentum, modulation_smoothed = update_one(modulation, modulation_moment, modulation_average, sums[0])
    attention_updated, attention_momentum, attention_smoothed = update_one(attention, attention_moment, attention_average, sums[1])
    outward_updated, outward_momentum, outward_smoothed = update_one(outward, outward_moment, outward_average, sums[2])
    expand_updated, expand_momentum, expand_smoothed = update_one(expand, expand_moment, expand_average, sums[3])
    shrink_updated, shrink_momentum, shrink_smoothed = update_one(shrink, shrink_moment, shrink_average, sums[4])
    return (block_output, input_gradient, conditioning_gradient, modulation_updated, modulation_momentum, modulation_smoothed, attention_updated, attention_momentum, attention_smoothed, outward_updated, outward_momentum, outward_smoothed, expand_updated, expand_momentum, expand_smoothed, shrink_updated, shrink_momentum, shrink_smoothed)
```

```python
from functools import partial
import math

import jax
import jax.numpy as jnp
from jax import lax
from jax.experimental import pallas as pl
from jax.experimental.pallas import tpu as pltpu
from jax.sharding import PartitionSpec as P

HEAD = 64
IMG = 1024


EPSILON = 1e-06
RATE = 0.0005
MOMENTUM = 0.9
AVERAGING = 0.8
MASKED = -1000000000.0
TILE = 256
PAIR = 2 * HEAD

F32 = jnp.float32
BF16 = jnp.bfloat16


def mm(left, right):
    return lax.dot_general(left, right, (((1,), (0,)), ((), ())), preferred_element_type=F32)


def mm_nt(left, right):
    return lax.dot_general(left, right, (((1,), (1,)), ((), ())), preferred_element_type=F32)


def mm_tn(left, right):
    return lax.dot_general(left, right, (((0,), (0,)), ((), ())), preferred_element_type=F32)


def fill(scratch, image_ref, text_ref):
    text = text_ref.shape[0]
    scratch[pl.ds(0, IMG), :] = image_ref[...]
    scratch[pl.ds(IMG, text), :] = text_ref[...]
    rest = scratch.shape[0] - IMG - text
    if rest:
        scratch[pl.ds(IMG + text, rest), :] = jnp.zeros((rest, scratch.shape[1]), scratch.dtype)


def open_slots(length, shape, axis):
    return lax.broadcasted_iota(jnp.int32, shape, axis) + IMG < length


def forward_kernel(sequence, length_ref, qi, ki, vi, qt, kt, vt, oi, ot, lse_ref, q_s, k_s, v_s, o_s):
    rows = q_s.shape[0]
    fill(q_s, qi, qt)
    fill(k_s, ki, kt)
    fill(v_s, vi, vt)
    lane = lax.broadcasted_iota(jnp.int32, (1, PAIR), 1)
    open_slot = open_slots(length_ref[sequence], (TILE, rows - IMG), 1)

    def one_tile(step, carry):
        start = pl.multiple_of(step * TILE, TILE)
        query = q_s[pl.ds(start, TILE), :]
        out = jnp.zeros((TILE, PAIR), F32)
        for half in range(2):
            mine = (lane // HEAD) == half
            mine_query = jnp.where(mine, query * 0.125, jnp.zeros_like(query))
            image = mm_nt(mine_query, k_s[pl.ds(0, IMG), :])
            text = mm_nt(mine_query, k_s[pl.ds(IMG, rows - IMG), :])
            text = jnp.where(open_slot, text, MASKED)
            peak = jnp.maximum(
                jnp.max(image, axis=1, keepdims=True), jnp.max(text, axis=1, keepdims=True)
            )
            image = jnp.exp(image - peak)
            text = jnp.exp(text - peak)
            total = jnp.sum(image, axis=1, keepdims=True) + jnp.sum(text, axis=1, keepdims=True)
            mixed = mm(image.astype(BF16), v_s[pl.ds(0, IMG), :])
            mixed += mm(text.astype(BF16), v_s[pl.ds(IMG, rows - IMG), :])
            out = jnp.where(mine, mixed * (1.0 / total), out)
            wide = jnp.broadcast_to(peak + jnp.log(total), (TILE, 128))
            lse_ref[0, pl.ds(half, 1), pl.ds(start, TILE)] = wide.T[:1]
        o_s[pl.ds(start, TILE), :] = out.astype(BF16)
        return carry

    lax.fori_loop(0, rows // TILE, one_tile, 0)
    oi[...] = o_s[pl.ds(0, IMG), :]
    ot[...] = o_s[pl.ds(IMG, ot.shape[0]), :]


def backward_kernel(
    sequence, length_ref, qi, ki, vi, di, qt, kt, vt, dt, lse_ref, gi, gt, q_s, k_s, v_s, d_s, kt_s, dq_s, dk_s, dv_s
):
    rows = q_s.shape[0]
    which = pl.program_id(1)

    @pl.when(which == 0)
    def compute():
        fill(q_s, qi, qt)
        fill(k_s, ki, kt)
        fill(v_s, vi, vt)
        fill(d_s, di, dt)
        kt_s[...] = k_s[...].T
        dk_s[...] = jnp.zeros_like(dk_s)
        dv_s[...] = jnp.zeros_like(dv_s)
        lane = lax.broadcasted_iota(jnp.int32, (1, PAIR), 1)
        open_slot = open_slots(length_ref[sequence], (rows - IMG, TILE), 0)

        def one_tile(step, carry):
            start = pl.multiple_of(step * TILE, TILE)
            query = q_s[pl.ds(start, TILE), :]
            upper = d_s[pl.ds(start, TILE), :]
            pieces = []
            for half in range(2):
                mine = (lane // HEAD) == half
                mine_query = jnp.where(mine, query * 0.125, jnp.zeros_like(query))
                mine_upper = jnp.where(mine, upper, jnp.zeros_like(upper))
                logsum = lse_ref[0, pl.ds(half, 1), pl.ds(start, TILE)]
                image = mm_nt(k_s[pl.ds(0, IMG), :], mine_query)
                text = mm_nt(k_s[pl.ds(IMG, rows - IMG), :], mine_query)
                text = jnp.where(open_slot, text, MASKED)
                image = jnp.exp(image - logsum)
                text = jnp.exp(text - logsum)
                up_image = mm_nt(v_s[pl.ds(0, IMG), :], mine_upper)
                up_text = mm_nt(v_s[pl.ds(IMG, rows - IMG), :], mine_upper)
                inner = jnp.sum(image * up_image, axis=0, keepdims=True)
                inner += jnp.sum(text * up_text, axis=0, keepdims=True)
                dv_s[pl.ds(0, IMG), :] += mm(image.astype(BF16), mine_upper)
                dv_s[pl.ds(IMG, rows - IMG), :] += mm(text.astype(BF16), mine_upper)
                d_image = (image * (up_image - inner)).astype(BF16)
                d_text = (text * (up_text - inner)).astype(BF16)
                dk_s[pl.ds(0, IMG), :] += mm(d_image, mine_query)
                dk_s[pl.ds(IMG, rows - IMG), :] += mm(d_text, mine_query)
                keys = kt_s[pl.ds(half * HEAD, HEAD), :]
                pieces.append(mm(keys[:, :IMG], d_image) + mm(keys[:, IMG:], d_text))
            across = jnp.concatenate(pieces, axis=0) * 0.125
            dq_s[pl.ds(start, TILE), :] = across.T.astype(BF16)
            return carry

        lax.fori_loop(0, rows // TILE, one_tile, 0)

    text_rows = gt.shape[0]

    @pl.when(which == 0)
    def write_query():
        gi[...] = dq_s[pl.ds(0, IMG), :]
        gt[...] = dq_s[pl.ds(IMG, text_rows), :]

    @pl.when(which == 1)
    def write_key():
        gi[...] = dk_s[pl.ds(0, IMG), :].astype(BF16)
        gt[...] = dk_s[pl.ds(IMG, text_rows), :].astype(BF16)

    @pl.when(which == 2)
    def write_value():
        gi[...] = dv_s[pl.ds(0, IMG), :].astype(BF16)
        gt[...] = dv_s[pl.ds(IMG, text_rows), :].astype(BF16)


def padded_rows(text):
    return -(-(IMG + text) // TILE) * TILE


def attend_forward(packed_image, packed_text, lengths, sequence):
    text = packed_text.shape[0]
    pairs = packed_image.shape[1] // (3 * PAIR)
    rows = padded_rows(text)

    def block(height, part):
        return pl.BlockSpec((height, PAIR), lambda j, _: (0, part * pairs + j))

    def result(height):
        return pl.BlockSpec((height, PAIR), lambda j, _: (0, j))

    return pl.pallas_call(
        partial(forward_kernel, sequence),
        grid_spec=pltpu.PrefetchScalarGridSpec(
            num_scalar_prefetch=1,
            grid=(pairs,),
            in_specs=[block(IMG, part) for part in range(3)]
            + [block(text, part) for part in range(3)],
            out_specs=[
                result(IMG),
                result(text),
                pl.BlockSpec((1, 2, rows), lambda j, _: (j, 0, 0)),
            ],
            scratch_shapes=[pltpu.VMEM((rows, PAIR), BF16)] * 4,
        ),
        out_shape=[
            jax.ShapeDtypeStruct((IMG, pairs * PAIR), BF16),
            jax.ShapeDtypeStruct((text, pairs * PAIR), BF16),
            jax.ShapeDtypeStruct((pairs, 2, rows), F32),
        ],
        compiler_params=pltpu.CompilerParams(vmem_limit_bytes=48 * 1024 * 1024),
        cost_estimate=pl.CostEstimate(
            flops=16 * pairs * rows * rows * PAIR,
            bytes_accessed=8 * pairs * rows * PAIR,
            transcendentals=2 * pairs * rows * rows,
        ),
        name="attend_forward",
    )(lengths, *([packed_image] * 3), *([packed_text] * 3))


def attend_backward(packed_image, packed_text, up_image, up_text, logsums, lengths, sequence):
    text = up_text.shape[0]
    pairs = packed_image.shape[1] // (3 * PAIR)
    rows = padded_rows(text)

    def block(height, part):
        return pl.BlockSpec((height, PAIR), lambda j, c, _: (0, part * pairs + j))

    def upper(height):
        return pl.BlockSpec((height, PAIR), lambda j, c, _: (0, j))

    return pl.pallas_call(
        partial(backward_kernel, sequence),
        grid_spec=pltpu.PrefetchScalarGridSpec(
            num_scalar_prefetch=1,
            grid=(pairs, 3),
            in_specs=[block(IMG, part) for part in range(3)]
            + [upper(IMG)]
            + [block(text, part) for part in range(3)]
            + [upper(text)]
            + [pl.BlockSpec((1, 2, rows), lambda j, c, _: (j, 0, 0))],
            out_specs=[
                pl.BlockSpec((IMG, PAIR), lambda j, c, _: (0, c * pairs + j)),
                pl.BlockSpec((text, PAIR), lambda j, c, _: (0, c * pairs + j)),
            ],
            scratch_shapes=[pltpu.VMEM((rows, PAIR), BF16)] * 4
            + [
                pltpu.VMEM((PAIR, rows), BF16),
                pltpu.VMEM((rows, PAIR), BF16),
                pltpu.VMEM((rows, PAIR), F32),
                pltpu.VMEM((rows, PAIR), F32),
            ],
        ),
        out_shape=[
            jax.ShapeDtypeStruct((IMG, 3 * pairs * PAIR), BF16),
            jax.ShapeDtypeStruct((text, 3 * pairs * PAIR), BF16),
        ],
        compiler_params=pltpu.CompilerParams(vmem_limit_bytes=48 * 1024 * 1024),
        cost_estimate=pl.CostEstimate(
            flops=40 * pairs * rows * rows * PAIR,
            bytes_accessed=16 * pairs * rows * PAIR,
            transcendentals=2 * pairs * rows * rows,
        ),
        name="attend_backward",
    )(
        lengths,
        *([packed_image] * 3),
        up_image,
        *([packed_text] * 3),
        up_text,
        logsums,
    )


def swap(values):
    return lax.ppermute(values, "tensor", [(0, 1), (1, 0)])


def tensor_gather(values, size, axis):
    if size == 2:
        other = swap(values)
        return jnp.where(
            lax.axis_index("tensor") == 0,
            jnp.concatenate([values, other], axis=axis),
            jnp.concatenate([other, values], axis=axis),
        )
    return lax.all_gather(values, "tensor", axis=axis, tiled=True)


def tensor_sum(values, size):
    if size == 2:
        return values + swap(values)
    return lax.psum(values, "tensor")


def tensor_scatter(image, text, size):
    values = jnp.concatenate([image, text], axis=0)
    rows = values.shape[0] // size
    if size == 2:
        me = lax.axis_index("tensor")
        away = lax.dynamic_slice_in_dim(values, (1 - me) * rows, rows, 0).astype(BF16)
        return lax.dynamic_slice_in_dim(values, me * rows, rows, 0) + swap(away).astype(F32)
    return lax.psum_scatter(values, "tensor", scatter_dimension=0, tiled=True)


def bit(k):
    return (lax.axis_index("dp") >> k) & 1


def flip(values, bits, groups):
    return lax.ppermute(values, "dp", [(index, index ^ bits) for index in range(groups)])


def over_pair(values, groups):
    return flip(values, 1, groups)


def count_bits(groups):
    return groups.bit_length() - 1


def small_order(groups):
    return [0] + list(range(count_bits(groups) - 1, 0, -1))


def small_gather(block, groups):
    for k in small_order(groups):
        block = jnp.concatenate([block, flip(block, 1 << k, groups)], axis=0)
    return block


def small_scatter(values, groups, pair):
    for k in reversed(small_order(groups)[1 if pair else 0 :]):
        half = values.shape[0] // 2
        values = values[:half] + flip(values[half:], 1 << k, groups)
    if pair:
        got = over_pair(values, groups)
        values = values + jnp.concatenate([got[1:], got[:1]], axis=0)
    return values


def same_side(groups):
    return [[index for index in range(groups) if index % 2 == side] for side in range(2)]


def pair_rows(image, text, kinds, groups):
    def halves(shard):
        return shard.reshape(shard.shape[0], kinds, 2, -1)

    split = jnp.concatenate([halves(image), halves(text)], axis=1)

    def side(which):
        part = lax.dynamic_index_in_dim(split, which, 2, keepdims=False)
        return part.reshape(part.shape[0], -1).astype(BF16)

    return side(bit(0)), over_pair(side(1 - bit(0)), groups)


def pair_join(mine, got):
    first = bit(0) == 0
    return jnp.concatenate([jnp.where(first, mine, got), jnp.where(first, got, mine)], axis=0)


def pair_gather(rows, groups):
    return lax.all_gather(rows, "dp", axis=0, tiled=True, axis_index_groups=same_side(groups))


def streams_of(weight):
    half = weight.shape[1] // 2
    return weight[:, :half], weight[:, half:]


def adjacent(first, second):
    return jnp.concatenate([first, second], axis=1)


def pair_scatter(grads, groups):
    return lax.psum_scatter(
        grads,
        "dp",
        scatter_dimension=0,
        tiled=True,
        axis_index_groups=same_side(groups),
    )


def own_shard(pair, kinds, groups):
    share = pair.shape[0] // 2
    mine = lax.dynamic_slice_in_dim(pair, bit(0) * share, share, 0)
    got = over_pair(lax.dynamic_slice_in_dim(pair, (1 - bit(0)) * share, share, 0), groups)
    first = bit(0) == 0
    halves = [jnp.where(first, mine, got), jnp.where(first, got, mine)]
    split = [half.reshape(share, 2, kinds, -1) for half in halves]
    return jnp.stack(split, axis=3).reshape(share, 2, -1).transpose(1, 0, 2).astype(F32)


def phase(*values):
    return lax.optimization_barrier(values)


def normalize(values):
    center = values - jnp.mean(values, axis=-1, keepdims=True)
    spread = jnp.mean(center * center, axis=-1, keepdims=True)
    scale = lax.rsqrt(spread + EPSILON)
    return center * scale, scale


def norm_back(normed, scale, grad):
    inner = jnp.mean(grad * normed, axis=-1, keepdims=True)
    return (grad - jnp.mean(grad, axis=-1, keepdims=True) - normed * inner) * scale


ROOT = math.sqrt(2.0 / math.pi)


def gelu_both(value):
    curve = jnp.tanh(ROOT * (value + 0.044715 * value * value * value))
    act = 0.5 * value * (1.0 + curve)
    slope = 0.5 * (1.0 + curve) + 0.5 * value * (1.0 - curve * curve) * ROOT * (
        1.0 + 3.0 * 0.044715 * value * value
    )
    return act, slope


def per_device(
    sizes,
    latents,
    conditioning,
    valid_length,
    cotangent,
    modulation,
    attention,
    outward,
    expand,
    shrink,
    modulation_moment,
    attention_moment,
    outward_moment,
    expand_moment,
    shrink_moment,
    modulation_average,
    attention_average,
    outward_average,
    expand_average,
    shrink_average,
):
    groups, tensors = sizes
    local_rows = latents.shape[1]
    width = latents.shape[2]
    share = width // groups
    heads_here = attention.shape[3] // HEAD
    spare = -heads_here % 4 * HEAD
    me_dp = lax.axis_index("dp")
    me_tensor = lax.axis_index("tensor")
    masters = (modulation, attention, outward, expand, shrink)
    moments = (modulation_moment, attention_moment, outward_moment, expand_moment, shrink_moment)
    averages = (
        modulation_average,
        attention_average,
        outward_average,
        expand_average,
        shrink_average,
    )

    def more_heads(values):
        return jnp.pad(values, ((0, 0),) * (values.ndim - 1) + ((0, spare),)) if spare else values

    def cut(local):
        rows = tensor_gather(local, tensors, 0)
        return rows[:IMG], rows[IMG:]

    attn_rows = pair_rows(more_heads(attention[0]), more_heads(attention[1]), 3, groups)
    out_rows = pair_rows(more_heads(outward[0].T), more_heads(outward[1].T), 1, groups)
    lengths = jnp.concatenate(
        [valid_length, over_pair(valid_length.astype(F32), groups).astype(jnp.int32)]
    )

    cond_value = conditioning.astype(F32)
    silu_cond, silu_pull = jax.vjp(jax.nn.silu, cond_value)
    cond_block = silu_cond.astype(BF16).reshape(1, -1, 128)
    cond_all = small_gather(cond_block, groups).reshape(groups, width)
    lengths, attn_rows, out_rows, cond_all = phase(lengths, attn_rows, out_rows, cond_all)
    heads_whole = pair_gather(adjacent(pair_join(*attn_rows), pair_join(*out_rows)), groups)
    cond_cols = lax.dynamic_slice_in_dim(cond_all, me_dp * share, share, 1)
    mod_low = modulation.astype(BF16)
    columns = modulation.shape[2]
    mod_part = jnp.einsum("sd,idm->sim", cond_cols, mod_low, preferred_element_type=F32)
    mod_sum = small_scatter(mod_part.reshape(groups, -1, 128), groups, True)
    mod_sum, latents_other = phase(mod_sum, over_pair(phase(latents[0], cond_all)[0], groups))
    expand_shards = phase(expand, mod_sum)[0]
    shrink_shards = phase(shrink, mod_sum)[0]
    expand_rows = pair_rows(expand_shards[0], expand_shards[1], 1, groups)
    shrink_rows = pair_rows(shrink_shards[0].T, shrink_shards[1].T, 1, groups)

    mods = tensor_gather(mod_sum.reshape(2, 2, columns), tensors, 2).reshape(2, 2, 6, width)
    both = range(2)
    image_row = me_tensor * local_rows + jnp.arange(local_rows)[:, None] < IMG
    here = [jnp.where(image_row, mods[0, 0, c][None], mods[0, 1, c][None]) for c in range(6)]
    residual, upstream = latents[0].astype(F32), cotangent[0].astype(F32)

    rows_one, packed = [], []
    for q, local in enumerate((latents[0], latents_other)):
        shaped = [
            normalize(rows.astype(F32))[0] * (1.0 + mods[q, i, 1]) + mods[q, i, 0]
            for i, rows in enumerate(cut(local))
        ]
        rows_one.append([values.astype(BF16) for values in shaped])
    rows_one, expand_rows, shrink_rows, upstream_other = phase(
        rows_one, expand_rows, shrink_rows, over_pair(phase(cotangent[0], mod_sum)[0], groups)
    )
    expand_whole = pair_gather(pair_join(*expand_rows), groups)
    shrink_whole = pair_gather(pair_join(*shrink_rows), groups)
    columns_q = 3 * (heads_here * HEAD + spare) // 2
    attn_w = streams_of(heads_whole[:, : 2 * columns_q])
    out_w = streams_of(heads_whole[:, 2 * columns_q :])
    packed = [[mm(rows_one[q][i], attn_w[i]).astype(BF16) for i in both] for q in both]

    *mixed_other, logs_other = attend_forward(*packed[1], lengths, 1)
    away = tensor_scatter(*[mm_nt(mixed_other[i], out_w[i]) for i in both], tensors).astype(BF16)
    away, packed[0] = phase(away, packed[0])
    down_in = []
    for q, local in enumerate((cotangent[0], upstream_other)):
        down = [mods[q, i, 5] * rows.astype(F32) for i, rows in enumerate(cut(local))]
        down_in.append([values.astype(BF16) for values in down])
    (*mixed_own, logs_own), away, down_in = phase(
        attend_forward(*packed[0], lengths, 0), over_pair(away, groups), down_in
    )

    branch_one = tensor_scatter(*[mm_nt(mixed_own[i], out_w[i]) for i in both], tensors)
    branch_one = branch_one + away.astype(F32)
    middle = residual + here[2] * branch_one
    normed_two, inv_two = normalize(middle)
    rows_two = (normed_two * (1.0 + here[4]) + here[3]).astype(BF16)

    def hidden_units(rows, weight):
        act, slope = gelu_both(mm(rows, weight))
        return act.astype(BF16), slope.astype(BF16)

    def hidden_back(down, weight, slope):
        return (mm(down, weight) * slope.astype(F32)).astype(BF16)

    expand_w = streams_of(expand_whole)
    rows_own = cut(rows_two)
    hidden_own = [hidden_units(rows_own[i], expand_w[i]) for i in both]
    shrink_own = [mm_tn(down_in[0][i], hidden_own[i][0]) for i in both]
    hidden_own, shrink_own, rows_other = phase(
        hidden_own, shrink_own, over_pair(rows_two, groups)
    )
    rows_other = cut(rows_other)
    hidden_other = [hidden_units(rows_other[i], expand_w[i]) for i in both]
    shrink_grad = [
        (shrink_own[i] + mm_tn(down_in[1][i], hidden_other[i][0])).astype(BF16) for i in both
    ]

    shrink_grad, hidden_own, hidden_other, shrink_whole = phase(
        shrink_grad, hidden_own, hidden_other, shrink_whole
    )
    shrink_w = streams_of(shrink_whole)
    shrink_sum = pair_scatter(adjacent(*shrink_grad), groups)

    back_other = [hidden_back(down_in[1][i], shrink_w[i], hidden_other[i][1]) for i in both]
    away = tensor_scatter(*[mm_nt(back_other[i], expand_w[i]) for i in both], tensors).astype(BF16)
    back_own = [hidden_back(down_in[0][i], shrink_w[i], hidden_own[i][1]) for i in both]
    back_own, back_other, away = phase(back_own, back_other, away)
    two_grad = tensor_scatter(*[mm_nt(back_own[i], expand_w[i]) for i in both], tensors)
    expand_grad = [
        (mm_tn(rows_own[i], back_own[i]) + mm_tn(rows_other[i], back_other[i])).astype(BF16)
        for i in both
    ]
    branch_away = tensor_scatter(
        *[mm_nt(hidden_other[i][0], shrink_w[i]) for i in both], tensors
    ).astype(BF16)
    two_grad, expand_grad, branch_away, away = phase(
        two_grad, expand_grad, branch_away, over_pair(away, groups)
    )
    expand_sum = pair_scatter(adjacent(*expand_grad), groups)
    two_grad = two_grad + away.astype(F32)
    middle_grad = upstream + norm_back(normed_two, inv_two, two_grad * (1.0 + here[4]))
    proj_in = (here[2] * middle_grad).astype(BF16)

    proj_own = cut(proj_in)
    mixed_grad = [mm(proj_own[i], out_w[i]).astype(BF16) for i in both]
    mixed_grad, proj_in = phase(mixed_grad, proj_in)
    grad_own, proj_other = phase(
        attend_backward(*packed[0], *mixed_grad, logs_own, lengths, 0),
        over_pair(proj_in, groups),
    )
    proj_other = cut(proj_other)
    mixed_grad = [mm(proj_other[i], out_w[i]).astype(BF16) for i in both]
    heads_own = [mm_tn(rows_one[0][i], grad_own[i]) for i in both]
    outward_grad = [
        (mm_tn(proj_own[i], mixed_own[i]) + mm_tn(proj_other[i], mixed_other[i])).astype(BF16)
        for i in both
    ]
    mixed_grad, branch_away, heads_own, outward_grad = phase(
        mixed_grad, branch_away, heads_own, outward_grad
    )
    grad_other, branch_away = phase(
        attend_backward(*packed[1], *mixed_grad, logs_other, lengths, 1),
        over_pair(branch_away, groups),
    )

    heads_grad = [
        (heads_own[i] + mm_tn(rows_one[1][i], grad_other[i])).astype(BF16) for i in both
    ]
    heads_grad = jnp.concatenate(
        [heads_grad[0], outward_grad[0], heads_grad[1], outward_grad[1]], axis=1
    )
    heads_grad, grad_other, grad_own, hidden_own = phase(
        heads_grad, grad_other, grad_own, hidden_own
    )
    heads_sum = pair_scatter(heads_grad, groups)
    away = tensor_scatter(*[mm_nt(grad_other[i], attn_w[i]) for i in both], tensors).astype(BF16)
    away, grad_own, hidden_own = phase(away, grad_own, hidden_own)
    one_grad = tensor_scatter(*[mm_nt(grad_own[i], attn_w[i]) for i in both], tensors)
    branch_two = tensor_scatter(*[mm_nt(hidden_own[i][0], shrink_w[i]) for i in both], tensors)
    branch_two = branch_two + branch_away.astype(F32)
    block_output = (middle + here[5] * branch_two).astype(BF16)
    one_grad, branch_two, away = phase(one_grad, branch_two, over_pair(away, groups))
    one_grad = one_grad + away.astype(F32)
    normed_one, inv_one = normalize(residual)
    latent_grad = middle_grad + norm_back(normed_one, inv_one, one_grad * (1.0 + here[1]))

    pieces = (
        one_grad,
        one_grad * normed_one,
        middle_grad * branch_one,
        two_grad,
        two_grad * normed_two,
        upstream * branch_two,
    )
    mod_grad = [jnp.sum(jnp.where(image_row, piece, 0.0), axis=0) for piece in pieces]
    mod_grad += [jnp.sum(jnp.where(image_row, 0.0, piece), axis=0) for piece in pieces]
    mod_grad = tensor_sum(jnp.stack(mod_grad), tensors).reshape(2, 6 * width)
    mod_columns = lax.dynamic_slice_in_dim(mod_grad, me_tensor * columns, columns, 1)
    mod_columns = mod_columns.astype(BF16).reshape(1, -1, 128)
    all_columns = small_gather(mod_columns, groups).astype(F32).reshape(groups, 2, columns)
    modulation_grad = jnp.einsum(
        "sd,sim->idm", cond_cols.astype(F32), all_columns, precision=lax.Precision.HIGHEST
    )
    cond_part = jnp.einsum(
        "sim,idm->sd", all_columns, mod_low.astype(F32), precision=lax.Precision.HIGHEST
    )
    cond_part = tensor_sum(cond_part, tensors)
    cond_wide = lax.dynamic_update_slice_in_dim(
        jnp.zeros((groups, width), F32), cond_part, me_dp * share, 1
    )
    cond_mine = small_scatter(cond_wide.reshape(groups, -1, 128), groups, False)
    cond_grad = silu_pull(cond_mine.reshape(1, width))[0]
    cond_share = width // tensors
    conditioning_grad = lax.dynamic_slice_in_dim(cond_grad, me_tensor * cond_share, cond_share, 1)

    shrink_grads = own_shard(shrink_sum, 1, groups).transpose(0, 2, 1)
    expand_grads = own_shard(expand_sum, 1, groups)
    heads_grads = own_shard(heads_sum, 4, groups).reshape(2, share, 4, -1)[..., : heads_here * HEAD]
    reduced = (
        modulation_grad,
        heads_grads[:, :, :3],
        heads_grads[:, :, 3].transpose(0, 2, 1),
        expand_grads,
        shrink_grads,
    )
    results = [block_output[None], latent_grad[None], conditioning_grad]
    for master, moment, average, summed in zip(masters, moments, averages, reduced):
        velocity = MOMENTUM * moment + summed
        updated = master - RATE * (summed + MOMENTUM * velocity)
        smoothed = AVERAGING * average + (1.0 - AVERAGING) * updated
        results += [updated, velocity, smoothed]
    return tuple(results)


def solution(mesh):
    tokens = P("dp", "tensor", None)
    by_rows = P(None, "dp", "tensor")
    by_heads = P(None, "dp", None, "tensor")
    by_columns = P(None, "tensor", "dp")
    weights = (by_rows, by_heads, by_columns, by_rows, by_columns)
    return jax.shard_map(
        partial(per_device, (mesh.shape["dp"], mesh.shape["tensor"])),
        mesh=mesh,
        in_specs=(tokens, P("dp", None), P("dp"), tokens) + 3 * weights,
        out_specs=(tokens, tokens, P("dp", "tensor"))
        + tuple(spec for spec in weights for _ in range(3)),
        check_vma=False,
    )
```
